256 devices in a mesh: tok: 4 (over y), row: 8 (over z_lo, core), col: 8 (over z_hi, x).
Axes of the slice: x: 4, y: 4, z: 8 (z_hi: 2, z_lo: 4; z = z_hi * 4 + z_lo), core: 2. Of those that a mesh axis runs over, the one named last changes fastest.
Arguments:
- pre_act: bfloat16 [1024, 49152], P(('tok', 'col'), 'row'), may hold values from -6 to 6
- out_grad: bfloat16 [1024, 12288], P('row', ('tok', 'col')), may hold values from -0.75 to 0.75
- down_weight: bfloat16 [49152, 12288], P('row', ('tok', 'col')), may hold values from -0.4375 to 0.4375
Outputs:
- grad_pre: bfloat16 [1024, 49152], P(('tok', 'col'), 'row')
- grad_down: bfloat16 [49152, 12288], P('row', ('tok', 'col'))
The draws below stay inside these ranges and needn't reach their ends.
All inputs are finite; a program needn't handle non-finite values.
Results may differ from the reference program's by a relative error of at most 0.0046.
Values may be sent and summed in bfloat16 or wider, within the bound.
No kernel may reach another device: no remote copies, remote signals or barrier semaphores. Data moves between devices by JAX's collectives and lax.ppermute only.
A program may use at most 128 MiB of HBM per device.

```python
import math
import jax
import jax.numpy as jnp

D = 12288
FF = 49152
TOKENS = 1024


def with_spikes(values, own_key, source, target, parts, factor):
    owner, partner = [(jnp.arange(values.shape[dim]) // (values.shape[dim] // parts)).reshape([-1 if axis == dim else 1 for axis in range(values.ndim)]) for dim in (source, target)]
    chosen = jax.random.permutation(own_key, parts)[partner]
    strong = (owner == chosen) | (owner == (partner + parts // 2) % parts)
    return jnp.where(strong, factor * values, values)


def level_of(own_key, extent, split, low, high):
    level, own = 1.0, jax.random.fold_in(own_key, 6)
    for position, shards_of in split:
        steps = jnp.exp(jax.random.uniform(jax.random.fold_in(own, position), (shards_of,), jnp.float32, low / len(split), high / len(split)))
        level = level * jnp.repeat(steps, extent[position] // shards_of).reshape([-1 if axis == position else 1 for axis in range(len(extent))])
    return level


def normal_values(own_key, extent, deviation, reach, shards=(), kind=jnp.bfloat16):
    level = level_of(own_key, extent, shards, -0.22, 0.18) if shards else 1.0
    values = jax.random.normal(own_key, extent, jnp.float32) * deviation * level
    return jnp.minimum(jnp.maximum(values, -reach), reach).astype(kind)


def noise_with(own_key, dims, width, bound, split, heavy, held_as=jnp.bfloat16):
    result = width * jax.random.normal(own_key, dims, jnp.float32)
    if split:
        result = result * level_of(own_key, dims, split, -0.22, 0.18)
    return jnp.clip(with_spikes(result, jax.random.fold_in(own_key, 3), *heavy), -bound, bound).astype(held_as)


def setup_inputs(seed: int = 0) -> dict:
    key_list = jax.random.split(jax.random.key(seed), 4)
    pre_act = normal_values(key_list[0], (TOKENS, FF), 1.5, 6.0, ((0, 32), (1, 8)))
    out_grad = noise_with(key_list[1], (TOKENS, D), 0.125, 0.75, ((0, 8), (1, 32)), (1, 0, 32, 2.75))
    down_weight = normal_values(key_list[2], (FF, D), (D // 64) ** -0.5, 0.4375, ((0, 8), (1, 32)))
    return dict(pre_act=pre_act, out_grad=out_grad, down_weight=down_weight)


root_coeff = math.sqrt(2.0 / math.pi)
cubic_coeff = 0.044715

def gelu_parts(widened):
    argument = root_coeff * (widened + cubic_coeff * widened * widened * widened)
    tangent = jnp.tanh(argument)
    gelu_value = 0.5 * widened * (1.0 + tangent)
    gelu_slope = 0.5 * (1.0 + tangent) + 0.5 * widened * (1.0 - tangent * tangent) * root_coeff * (1.0 + 3.0 * cubic_coeff * widened * widened)
    return (gelu_value, gelu_slope)

def reference(pre_act, out_grad, down_weight):
    widened = pre_act.astype(jnp.float32)
    gelu_value, gelu_slope = gelu_parts(widened)
    activation = gelu_value.astype(jnp.bfloat16)
    grad_act = jnp.dot(out_grad, down_weight.T, preferred_element_type=jnp.float32)
    grad_pre = (grad_act * gelu_slope).astype(jnp.bfloat16)
    grad_down = jnp.dot(activation.T, out_grad, preferred_element_type=jnp.float32).astype(jnp.bfloat16)
    return (grad_pre, grad_down)
```

```python
import math

import jax
import jax.numpy as jnp
from jax import lax
from jax.sharding import Mesh, PartitionSpec as P

root_coeff = math.sqrt(2.0 / math.pi)
cubic_coeff = 0.044715
PLANE = ("y", "x")


def gelu_parts(widened):
    argument = root_coeff * (widened + cubic_coeff * widened * widened * widened)
    tangent = jnp.tanh(argument)
    gelu_value = 0.5 * widened * (1.0 + tangent)
    gelu_slope = 0.5 * (1.0 + tangent) + 0.5 * widened * (1.0 - tangent * tangent) * root_coeff * (
        1.0 + 3.0 * cubic_coeff * widened * widened
    )
    return (gelu_value, gelu_slope)


def shift(block, axis, step):
    size = lax.axis_size(axis)
    return lax.ppermute(block, axis, [(i, (i + step) % size) for i in range(size)])


def turned(blocks, axis, dim):
    size = blocks.shape[dim]
    doubled = jnp.concatenate([blocks, blocks], axis=dim)
    return lax.dynamic_slice_in_dim(doubled, lax.axis_index(axis), size, dim)


def share(rows, weight):
    return lax.dot_general(rows, weight, (((1,), (1,)), ((), ())), preferred_element_type=jnp.float32)


def ring_sum(parts, axis):
    half = parts.rows // 2
    to_right = shift(parts(2, 0, half).astype(jnp.bfloat16), axis, 1)
    to_left = shift(parts(2, half, 2 * half).astype(jnp.bfloat16), axis, -1)
    right = parts(1, 0, 2 * half)
    right = jnp.concatenate([right[:half] + to_right.astype(jnp.float32), right[half:]], axis=0)
    left = parts(3, 0, 2 * half)
    left = jnp.concatenate([left[:half], left[half:] + to_left.astype(jnp.float32)], axis=0)
    from_left = shift(right.astype(jnp.bfloat16), axis, 1)
    from_right = shift(left.astype(jnp.bfloat16), axis, -1)
    return parts(0, 0, 2 * half) + from_left.astype(jnp.float32) + from_right.astype(jnp.float32)


class Shares:
    def __init__(self, blocks, weight):
        self.blocks, self.weight, self.rows = blocks, weight, blocks[0].shape[0]

    def __call__(self, ahead, low, high):
        return share(self.blocks[ahead][low:high], self.weight)


def second_sum(total, axis):
    narrow = total.astype(jnp.bfloat16)
    sums = []
    for z in range(total.shape[0])[::-1]:
        got = [shift(narrow[z, d], axis, d if d < 3 else -1) for d in (1, 3, 2)]
        sums.append(total[z, 0] + sum(g.astype(jnp.float32) for g in got))
    return sums


def stage_one(grad, weight):
    ny, nz, nx, tokens, width = grad.shape
    half = weight.shape[0] // 2
    by_y = [grad[d].reshape(-1, width) for d in range(ny)]
    by_x = [jnp.swapaxes(grad[:, :, d], 0, 1).reshape(-1, width) for d in range(nx)]
    low = ring_sum(Shares(by_y, weight[:half]), "y")
    high = ring_sum(Shares(by_x, weight[half:]), "x")
    return low.reshape(nz, nx, tokens, half), high.reshape(nz, ny, tokens, half)


def shards(pre_act, out_grad, down_weight):
    tokens, hidden = pre_act.shape
    width = out_grad.shape[1]
    widened = pre_act.astype(jnp.float32)
    gelu_value, gelu_slope = gelu_parts(widened)
    activation = gelu_value.astype(jnp.bfloat16)
    swap = [(0, 1), (1, 0)]
    activation, out_grad = lax.optimization_barrier((activation, out_grad))
    mine = lax.all_gather(activation, PLANE, axis=0, tiled=True)
    grad_all = lax.all_gather(out_grad, ("zl", "c"), axis=0, tiled=True)
    blocks = grad_all.reshape(4, 2, 4, tokens, width)
    by_z = turned(blocks, "zh", 1)
    late, by_z = lax.optimization_barrier((activation, by_z))
    other = lax.ppermute(late, "zh", swap)
    relative = turned(turned(by_z, "y", 0), "x", 2)
    theirs = lax.all_gather(other, PLANE, axis=0, tiled=True)
    g0 = by_z[:, 0].reshape(-1, width)
    g1 = by_z[:, 1].reshape(-1, width)
    dn = (((0,), (0,)), ((), ()))
    grad_down = lax.dot_general(mine, g0, dn, preferred_element_type=jnp.float32) + lax.dot_general(
        theirs, g1, dn, preferred_element_type=jnp.float32
    )
    grad_down = grad_down.astype(jnp.bfloat16)
    low, high = stage_one(relative[:, 1:], down_weight)
    low2, high2 = stage_one(relative[:, :1], down_weight)
    low_away, = second_sum(low, "x")
    high_away, = second_sum(high, "y")
    low_home, = second_sum(low2, "x")
    high_home, = second_sum(high2, "y")
    away = jnp.concatenate([low_away, high_away], axis=1)
    received = lax.ppermute(away.astype(jnp.bfloat16), "zh", swap)
    home = jnp.concatenate([low_home, high_home], axis=1)
    grad_act = home + received.astype(jnp.float32)
    grad_pre = (grad_act * gelu_slope).astype(jnp.bfloat16)
    return (grad_pre, grad_down)


def solution(mesh):
    split = Mesh(mesh.devices.reshape(4, 4, 2, 2, 4), ("y", "zl", "c", "zh", "x"))
    tokens, hidden = ("y", "zh", "x"), ("zl", "c")
    return jax.shard_map(
        shards,
        mesh=split,
        in_specs=(P(tokens, hidden), P(hidden, tokens), P(hidden, tokens)),
        out_specs=(P(tokens, hidden), P(hidden, tokens)),
        check_vma=False,
    )
```

```python
import math

import jax
import jax.numpy as jnp
from jax import lax
from jax.sharding import Mesh, PartitionSpec as P

root_coeff = math.sqrt(2.0 / math.pi)
cubic_coeff = 0.044715
PLANE = ("y", "x")


def gelu_parts(widened):
    argument = root_coeff * (widened + cubic_coeff * widened * widened * widened)
    tangent = jnp.tanh(argument)
    gelu_value = 0.5 * widened * (1.0 + tangent)
    gelu_slope = 0.5 * (1.0 + tangent) + 0.5 * widened * (1.0 - tangent * tangent) * root_coeff * (
        1.0 + 3.0 * cubic_coeff * widened * widened
    )
    return (gelu_value, gelu_slope)


def shift(block, axis, step):
    size = lax.axis_size(axis)
    return lax.ppermute(block, axis, [(i, (i + step) % size) for i in range(size)])


def turned(blocks, axis, dim):
    size = blocks.shape[dim]
    doubled = jnp.concatenate([blocks, blocks], axis=dim)
    return lax.dynamic_slice_in_dim(doubled, lax.axis_index(axis), size, dim)


def share(rows, weight):
    return lax.dot_general(rows, weight, (((1,), (1,)), ((), ())), preferred_element_type=jnp.float32)


def after(value, *others):
    return lax.optimization_barrier((value, *others))[0]


def wide(value):
    return value.astype(jnp.float32)


def narrow(value):
    return value.astype(jnp.bfloat16)


def far_send(blocks, weight, axis):
    half = blocks[2].shape[0] // 2
    right = shift(narrow(share(blocks[2][:half], weight)), axis, 1)
    left = shift(narrow(share(blocks[2][half:], weight)), axis, -1)
    return right, left


def near_operands(blocks, weight, got):
    half = blocks[1].shape[0] // 2
    right = share(blocks[1], weight)
    right = narrow(jnp.concatenate([right[:half] + wide(got[0]), right[half:]], axis=0))
    left = share(blocks[3], weight)
    left = narrow(jnp.concatenate([left[:half], left[half:] + wide(got[1])], axis=0))
    return right, left


def near_send(operands, axis):
    return shift(operands[0], axis, 1), shift(operands[1], axis, -1)


def own_sum(blocks, weight, got):
    return share(blocks[0], weight) + wide(got[0]) + wide(got[1])


def split_blocks(grad):
    width = grad.shape[-1]
    by_y = [grad[d].reshape(-1, width) for d in range(4)]
    by_x = [grad[:, d].reshape(-1, width) for d in range(4)]
    return by_y, by_x


def second_sum(total, axis):
    blocks = total.reshape(4, -1, total.shape[-1])
    sent = narrow(blocks)
    got = [shift(sent[d], axis, d if d < 3 else -1) for d in (1, 3, 2)]
    return blocks[0] + wide(got[0]) + wide(got[1]) + wide(got[2])


def shards(pre_act, out_grad, down_weight):
    tokens, hidden = pre_act.shape
    width = out_grad.shape[1]
    widened = pre_act.astype(jnp.float32)
    gelu_value, gelu_slope = gelu_parts(widened)
    activation = gelu_value.astype(jnp.bfloat16)
    swap = [(0, 1), (1, 0)]
    activation, out_grad = lax.optimization_barrier((activation, out_grad))
    mine = lax.all_gather(activation, PLANE, axis=0, tiled=True)
    grad_all = lax.all_gather(out_grad, ("zl", "c"), axis=0, tiled=True)
    blocks = grad_all.reshape(4, 2, 4, tokens, width)
    by_z = turned(blocks, "zh", 1)
    late, by_z = lax.optimization_barrier((activation, by_z))
    other = lax.ppermute(late, "zh", swap)
    relative = turned(turned(by_z, "y", 0), "x", 2)
    theirs = lax.all_gather(other, PLANE, axis=0, tiled=True)
    g0 = by_z[:, 0].reshape(-1, width)
    g1 = by_z[:, 1].reshape(-1, width)
    dn = (((0,), (0,)), ((), ()))
    first = narrow(lax.dot_general(mine, g0, dn, preferred_element_type=jnp.float32))
    grad_down = narrow(lax.dot_general(theirs, g1, dn, preferred_element_type=jnp.float32) + wide(first))
    half = hidden // 2
    weights = (down_weight[:half], down_weight[half:])
    axes = ("y", "x")
    away = split_blocks(relative[:, 1])
    away_far = [far_send(away[i], weights[i], axes[i]) for i in (0, 1)]
    away_near = [near_operands(away[i], weights[i], away_far[i]) for i in (0, 1)]
    away_got = [near_send(away_near[i], axes[i]) for i in (0, 1)]
    home_rel = after(relative[:, 0], away_near[0][0])
    home = split_blocks(home_rel)
    home_far = [far_send(home[i], weights[i], axes[i]) for i in (0, 1)]
    own = [[after(away[i][0], away_far[i][0])] for i in (0, 1)]
    away_sum = [own_sum(own[i], weights[i], away_got[i]) for i in (0, 1)]
    home = [[after(home[i][d], away_got[i][0]) if d != 2 else home[i][d] for d in range(4)] for i in (0, 1)]
    home_near = [near_operands(home[i], weights[i], home_far[i]) for i in (0, 1)]
    home_got = [near_send(home_near[i], axes[i]) for i in (0, 1)]
    home_sum = [own_sum(home[i], weights[i], home_got[i]) for i in (0, 1)]
    away_out = jnp.concatenate([second_sum(away_sum[0], "x"), second_sum(away_sum[1], "y")], axis=1)
    received = lax.ppermute(narrow(away_out), "zh", swap)
    home = jnp.concatenate([second_sum(home_sum[0], "x"), second_sum(home_sum[1], "y")], axis=1)
    grad_act = home + received.astype(jnp.float32)
    grad_pre = (grad_act * gelu_slope).astype(jnp.bfloat16)
    return (grad_pre, grad_down)


def solution(mesh):
    split = Mesh(mesh.devices.reshape(4, 4, 2, 2, 4), ("y", "zl", "c", "zh", "x"))
    tokens, hidden = ("y", "zh", "x"), ("zl", "c")
    return jax.shard_map(
        shards,
        mesh=split,
        in_specs=(P(tokens, hidden), P(hidden, tokens), P(hidden, tokens)),
        out_specs=(P(tokens, hidden), P(hidden, tokens)),
        check_vma=False,
    )
```

```python
import math

import jax
import jax.numpy as jnp
from jax import lax
from jax.sharding import Mesh, PartitionSpec as P

root_coeff = math.sqrt(2.0 / math.pi)
cubic_coeff = 0.044715
PLANE = ("y", "x")


def gelu_parts(widened):
    argument = root_coeff * (widened + cubic_coeff * widened * widened * widened)
    tangent = jnp.tanh(argument)
    gelu_value = 0.5 * widened * (1.0 + tangent)
    gelu_slope = 0.5 * (1.0 + tangent) + 0.5 * widened * (1.0 - tangent * tangent) * root_coeff * (
        1.0 + 3.0 * cubic_coeff * widened * widened
    )
    return (gelu_value, gelu_slope)


def shift(block, axis, step):
    size = lax.axis_size(axis)
    return lax.ppermute(block, axis, [(i, (i + step) % size) for i in range(size)])


def turned(blocks, axis, dim):
    size = blocks.shape[dim]
    doubled = jnp.concatenate([blocks, blocks], axis=dim)
    return lax.dynamic_slice_in_dim(doubled, lax.axis_index(axis), size, dim)


def share(rows, weight):
    return lax.dot_general(rows, weight, (((1,), (1,)), ((), ())), preferred_element_type=jnp.float32)


def ring_sum(parts, axis):
    half = parts.rows // 2
    to_right = shift(parts(2, 0, half).astype(jnp.bfloat16), axis, 1)
    to_left = shift(parts(2, half, 2 * half).astype(jnp.bfloat16), axis, -1)
    right = parts(1, 0, 2 * half)
    right = jnp.concatenate([right[:half] + to_right.astype(jnp.float32), right[half:]], axis=0)
    left = parts(3, 0, 2 * half)
    left = jnp.concatenate([left[:half], left[half:] + to_left.astype(jnp.float32)], axis=0)
    from_left = shift(right.astype(jnp.bfloat16), axis, 1)
    from_right = shift(left.astype(jnp.bfloat16), axis, -1)
    return parts(0, 0, 2 * half) + from_left.astype(jnp.float32) + from_right.astype(jnp.float32)


class Shares:
    def __init__(self, blocks, weight):
        self.blocks, self.weight, self.rows = blocks, weight, blocks[0].shape[0]

    def __call__(self, ahead, low, high):
        return share(self.blocks[ahead][low:high], self.weight)


def second_sum(total, axis):
    narrow = total.astype(jnp.bfloat16)
    sums = []
    for z in range(total.shape[0])[::-1]:
        got = [shift(narrow[z, d], axis, d if d < 3 else -1) for d in (1, 3, 2)]
        sums.append(total[z, 0] + sum(g.astype(jnp.float32) for g in got))
    return sums


def stage_one(grad, weight):
    ny, nz, nx, tokens, width = grad.shape
    half = weight.shape[0] // 2
    by_y = [grad[d].reshape(-1, width) for d in range(ny)]
    by_x = [jnp.swapaxes(grad[:, :, d], 0, 1).reshape(-1, width) for d in range(nx)]
    low = ring_sum(Shares(by_y, weight[:half]), "y")
    high = ring_sum(Shares(by_x, weight[half:]), "x")
    return low.reshape(nz, nx, tokens, half), high.reshape(nz, ny, tokens, half)


def shards(pre_act, out_grad, down_weight):
    tokens, hidden = pre_act.shape
    width = out_grad.shape[1]
    widened = pre_act.astype(jnp.float32)
    gelu_value, gelu_slope = gelu_parts(widened)
    activation = gelu_value.astype(jnp.bfloat16)
    swap = [(0, 1), (1, 0)]
    activation, out_grad = lax.optimization_barrier((activation, out_grad))
    mine = lax.all_gather(activation, PLANE, axis=0, tiled=True)
    grad_all = lax.all_gather(out_grad, ("zl", "c"), axis=0, tiled=True)
    blocks = grad_all.reshape(4, 2, 4, tokens, width)
    by_z = turned(blocks, "zh", 1)
    late, by_z = lax.optimization_barrier((activation, by_z))
    other = lax.ppermute(late, "zh", swap)
    relative = turned(turned(by_z, "y", 0), "x", 2)
    theirs = lax.all_gather(other, PLANE, axis=0, tiled=True)
    g0 = by_z[:, 0].reshape(-1, width)
    g1 = by_z[:, 1].reshape(-1, width)
    dn = (((0,), (0,)), ((), ()))
    first = lax.dot_general(mine, g0, dn, preferred_element_type=jnp.float32).astype(jnp.bfloat16)
    grad_down = lax.dot_general(theirs, g1, dn, preferred_element_type=jnp.float32) + first.astype(jnp.float32)
    grad_down = grad_down.astype(jnp.bfloat16)
    low, high = stage_one(relative[:, 1:], down_weight)
    low2, high2 = stage_one(relative[:, :1], down_weight)
    low_away, = second_sum(low, "x")
    high_away, = second_sum(high, "y")
    low_home, = second_sum(low2, "x")
    high_home, = second_sum(high2, "y")
    away = jnp.concatenate([low_away, high_away], axis=1)
    received = lax.ppermute(away.astype(jnp.bfloat16), "zh", swap)
    home = jnp.concatenate([low_home, high_home], axis=1)
    grad_act = home + received.astype(jnp.float32)
    grad_pre = (grad_act * gelu_slope).astype(jnp.bfloat16)
    return (grad_pre, grad_down)


def solution(mesh):
    split = Mesh(mesh.devices.reshape(4, 4, 2, 2, 4), ("y", "zl", "c", "zh", "x"))
    tokens, hidden = ("y", "zh", "x"), ("zl", "c")
    return jax.shard_map(
        shards,
        mesh=split,
        in_specs=(P(tokens, hidden), P(hidden, tokens), P(hidden, tokens)),
        out_specs=(P(tokens, hidden), P(hidden, tokens)),
        check_vma=False,
    )
```

```python
import math

import jax
import jax.numpy as jnp
from jax import lax
from jax.sharding import Mesh, PartitionSpec as P

root_coeff = math.sqrt(2.0 / math.pi)
cubic_coeff = 0.044715
PLANE = ("y", "x")


def gelu_parts(widened):
    argument = root_coeff * (widened + cubic_coeff * widened * widened * widened)
    tangent = jnp.tanh(argument)
    gelu_value = 0.5 * widened * (1.0 + tangent)
    gelu_slope = 0.5 * (1.0 + tangent) + 0.5 * widened * (1.0 - tangent * tangent) * root_coeff * (
        1.0 + 3.0 * cubic_coeff * widened * widened
    )
    return (gelu_value, gelu_slope)


def shift(block, axis, step):
    size = lax.axis_size(axis)
    return lax.ppermute(block, axis, [(i, (i + step) % size) for i in range(size)])


def turned(blocks, axis, dim):
    size = blocks.shape[dim]
    doubled = jnp.concatenate([blocks, blocks], axis=dim)
    return lax.dynamic_slice_in_dim(doubled, lax.axis_index(axis), size, dim)


def share(rows, weight):
    return lax.dot_general(rows, weight, (((1,), (1,)), ((), ())), preferred_element_type=jnp.float32)


def ring_sum(parts, axis):
    half = parts.rows // 2
    to_right = shift(parts(2, 0, half).astype(jnp.bfloat16), axis, 1)
    to_left = shift(parts(2, half, 2 * half).astype(jnp.bfloat16), axis, -1)
    right = parts(1, 0, 2 * half)
    right = jnp.concatenate([right[:half] + to_right.astype(jnp.float32), right[half:]], axis=0)
    left = parts(3, 0, 2 * half)
    left = jnp.concatenate([left[:half], left[half:] + to_left.astype(jnp.float32)], axis=0)
    from_left = shift(right.astype(jnp.bfloat16), axis, 1)
    from_right = shift(left.astype(jnp.bfloat16), axis, -1)
    return parts(0, 0, 2 * half) + from_left.astype(jnp.float32) + from_right.astype(jnp.float32)


class Shares:
    def __init__(self, blocks, weight):
        self.blocks, self.weight, self.rows = blocks, weight, blocks[0].shape[0]

    def __call__(self, ahead, low, high):
        return share(self.blocks[ahead][low:high], self.weight)


def second_sum(total, axis):
    narrow = total.astype(jnp.bfloat16)
    sums = []
    for z in range(total.shape[0])[::-1]:
        got = [shift(narrow[z, d], axis, d if d < 3 else -1) for d in (1, 3, 2)]
        sums.append(total[z, 0] + sum(g.astype(jnp.float32) for g in got))
    return sums


def stage_one(grad, weight):
    ny, nz, nx, tokens, width = grad.shape
    half = weight.shape[0] // 2
    by_y = [grad[d].reshape(-1, width) for d in range(ny)]
    by_x = [jnp.swapaxes(grad[:, :, d], 0, 1).reshape(-1, width) for d in range(nx)]
    low = ring_sum(Shares(by_y, weight[:half]), "y")
    high = ring_sum(Shares(by_x, weight[half:]), "x")
    return low.reshape(nz, nx, tokens, half), high.reshape(nz, ny, tokens, half)


def shards(pre_act, out_grad, down_weight):
    tokens, hidden = pre_act.shape
    width = out_grad.shape[1]
    widened = pre_act.astype(jnp.float32)
    gelu_value, gelu_slope = gelu_parts(widened)
    activation = gelu_value.astype(jnp.bfloat16)
    swap = [(0, 1), (1, 0)]
    activation, out_grad = lax.optimization_barrier((activation, out_grad))
    mine = lax.all_gather(activation, PLANE, axis=0, tiled=True)
    grad_all = lax.all_gather(out_grad, ("zl", "c"), axis=0, tiled=True)
    blocks = grad_all.reshape(4, 2, 4, tokens, width)
    by_z = turned(blocks, "zh", 1)
    late, by_z = lax.optimization_barrier((activation, by_z))
    other = lax.ppermute(late, "zh", swap)
    relative = turned(turned(by_z, "y", 0), "x", 2)
    theirs = lax.all_gather(other, PLANE, axis=0, tiled=True)
    g0 = by_z[:, 0].reshape(-1, width)
    g1 = by_z[:, 1].reshape(-1, width)
    dn = (((0,), (0,)), ((), ()))
    first = lax.dot_general(mine, g0, dn, preferred_element_type=jnp.float32).astype(jnp.bfloat16)
    low, high = stage_one(relative[:, 1:], down_weight)
    low2, high2 = stage_one(relative[:, :1], down_weight)
    low2, first = lax.optimization_barrier((low2, first))
    low_away, = second_sum(low, "x")
    high_away, = second_sum(high, "y")
    low_home, = second_sum(low2, "x")
    high_home, = second_sum(high2, "y")
    grad_down = lax.dot_general(theirs, g1, dn, preferred_element_type=jnp.float32) + first.astype(jnp.float32)
    grad_down = grad_down.astype(jnp.bfloat16)
    away = jnp.concatenate([low_away, high_away], axis=1)
    received = lax.ppermute(away.astype(jnp.bfloat16), "zh", swap)
    home = jnp.concatenate([low_home, high_home], axis=1)
    grad_act = home + received.astype(jnp.float32)
    grad_pre = (grad_act * gelu_slope).astype(jnp.bfloat16)
    return (grad_pre, grad_down)


def solution(mesh):
    split = Mesh(mesh.devices.reshape(4, 4, 2, 2, 4), ("y", "zl", "c", "zh", "x"))
    tokens, hidden = ("y", "zh", "x"), ("zl", "c")
    return jax.shard_map(
        shards,
        mesh=split,
        in_specs=(P(tokens, hidden), P(hidden, tokens), P(hidden, tokens)),
        out_specs=(P(tokens, hidden), P(hidden, tokens)),
        check_vma=False,
    )
```
